512 devices in a mesh: chan: 32 (over z_lo, x), tm: 16 (over z_hi, y, core).
Axes of the slice: x: 4, y: 4, z: 16 (z_hi: 2, z_lo: 8; z = z_hi * 8 + z_lo), core: 2. Of those that a mesh axis runs over, the one named last changes fastest.
Arguments:
- samples: bfloat16 [8192, 65536], P('chan', 'tm'), as said below
Outputs:
- coherence: float32 [16, 4, 2, 8192, 256], P('tm', None, None, 'chan')
Inputs may be any that keep to these rules, and one draw needn't show every extreme that they name: Real-valued samples of the fibre's channels.
All inputs are finite; a program needn't handle non-finite values.
Results may differ from the reference program's by a relative error of at most 0.00095.
Values may be sent and summed in bfloat16 or wider, within the bound.
A program may use at most 64 MiB of HBM per device.

```python
import math
import jax
import jax.numpy as jnp
from jax import lax

CHAN_DEV = 256
NFFT = 256
TAPS = 16
ROUNDS = 3
C = 8192
BINS = 128
BANDS = 16
BAND = 8
SUBS = 256
NSAMP = 65536
N_CHAN = 32


def draw_samples(key, part):
    keys = jax.random.split(key, 4)
    coupling = jax.random.uniform(keys[0], (C, 1), jnp.float32, -1.5, 1.5)
    common = jnp.clip(jax.random.normal(keys[1], (1, NSAMP), jnp.float32), -4.0, 4.0)
    noise = jnp.clip(jax.random.normal(keys[2], (C, NSAMP), jnp.float32), -4.0, 4.0)
    levels = jnp.exp(jax.random.uniform(keys[3], (C, SUBS), jnp.float32, 0.0, math.log(10.0)))
    levels = jnp.repeat(levels, NFFT, axis=1)
    return (levels * (coupling * common + noise)).astype(jnp.bfloat16)


def setup_inputs(seed: int = 0) -> dict:
    seeds = jax.random.split(jax.random.key(seed), 2)
    return {
        "samples": draw_samples(jax.random.fold_in(seeds[1], 71), 0),
    }


epsilon = 1e-06

def prototype():
    length = TAPS * NFFT
    sample_index = jnp.arange(length, dtype=jnp.float32)
    centred = (sample_index + 0.5 - 0.5 * length) / NFFT
    window = jnp.sinc(centred) * (0.5 + 0.5 * jnp.cos(2.0 * math.pi * centred / TAPS))
    return window.reshape(TAPS, NFFT)

def transform_table():
    frequency = jnp.arange(BINS, dtype=jnp.int32)[:, None]
    position = jnp.arange(NFFT, dtype=jnp.int32)[None, :]
    phases = (frequency * position % NFFT).astype(jnp.float32) * (2.0 * math.pi / NFFT)
    return jnp.concatenate([jnp.cos(phases), -jnp.sin(phases)], 0).astype(jnp.bfloat16)

def filter_frames(extended, taps_table, sub_count):
    summed = jnp.zeros((extended.shape[0], sub_count, extended.shape[2]), jnp.float32)
    for offset in range(TAPS):
        summed = summed + taps_table[offset] * extended[:, offset:offset + sub_count, :].astype(jnp.float32)
    return summed.astype(jnp.bfloat16)

def reference(samples):
    taps_table = prototype()
    fourier = transform_table()
    entire = samples.reshape(N_CHAN, CHAN_DEV, SUBS, NFFT)
    leading = jnp.zeros((N_CHAN, CHAN_DEV, TAPS - 1, NFFT), jnp.bfloat16)
    padded = jnp.concatenate([leading, entire], axis=2)

    def block_white(channels):
        frames = filter_frames(channels, taps_table, SUBS)
        spectra = jnp.einsum('fn,csn->fsc', fourier.astype(jnp.float32), frames.astype(jnp.float32))
        spectra = spectra.astype(jnp.bfloat16).reshape(2, BINS, SUBS, CHAN_DEV).astype(jnp.float32)
        power_mean = lax.optimization_barrier(jnp.mean(spectra[0] * spectra[0] + spectra[1] * spectra[1], axis=1))
        return (spectra * lax.rsqrt(power_mean + epsilon)[None, :, None, :]).astype(jnp.bfloat16)
    whitened = lax.map(block_white, padded)
    banded = whitened.reshape(N_CHAN, 2, BANDS, BAND * SUBS, CHAN_DEV)

    def block_cross(block_index):
        own_block = lax.dynamic_index_in_dim(banded, block_index, 0, keepdims=False).astype(jnp.float32)
        collected = []
        for distance in range(ROUNDS + 1):
            where = ((block_index - distance) % N_CHAN).astype(jnp.int32)
            partner = lax.dynamic_index_in_dim(banded, where, 0, keepdims=False).astype(jnp.float32)
            real_part = jnp.einsum('tkc,tkd->tcd', own_block[0], partner[0]) + jnp.einsum('tkc,tkd->tcd', own_block[1], partner[1])
            imag_part = jnp.einsum('tkc,tkd->tcd', own_block[1], partner[0]) - jnp.einsum('tkc,tkd->tcd', own_block[0], partner[1])
            collected.append(jnp.stack([real_part, imag_part], 1))
        return jnp.stack(collected, 1) / SUBS
    coherences = lax.map(block_cross, jnp.arange(N_CHAN, dtype=jnp.int32))
    return jnp.transpose(coherences, (1, 2, 3, 0, 4, 5)).reshape(BANDS, ROUNDS + 1, 2, C, CHAN_DEV)
```

```python
import math

import jax
import jax.numpy as jnp
import numpy as np
from jax import lax
from jax.experimental import pallas as pl
from jax.experimental.pallas import tpu as pltpu
from jax.sharding import PartitionSpec as P

NFFT = 256
TAPS = 16
BINS = 128
CHANNELS = 256
GROUP = 8
LOCAL = 16
CHUNKS = 8
PER = LOCAL // CHUNKS
SLOTS = 16
EARLY = 7
ROW = 4

epsilon = 1e-06
MESH = pl.DeviceIdType.MESH


def prototype():
    centred = (np.arange(TAPS * NFFT, dtype=np.float64) + 0.5 - 0.5 * TAPS * NFFT) / NFFT
    window = np.sinc(centred) * (0.5 + 0.5 * np.cos(2.0 * math.pi * centred / TAPS))
    table = window.reshape(TAPS, 1, NFFT).astype(np.float32)
    return np.broadcast_to(table, (TAPS, 8, NFFT)).copy()


def transform_table():
    frequency = np.arange(BINS)[:, None]
    phases = (frequency * np.arange(NFFT)[None, :] % NFFT) * (2.0 * math.pi / NFFT)
    parts = np.stack([np.cos(phases), -np.sin(phases)]).reshape(2, 16, 8, NFFT)
    return jnp.asarray(parts.transpose(1, 0, 2, 3).reshape(2 * BINS, NFFT), jnp.bfloat16)


def kernel(samples, proto, fourier, out, frames, outgoing, incoming, both, crossing, spill, others,
           power, white, turned, y_send, y_recv, self_sem, z_send, z_recv, spill_send, spill_recv,
           up_send, up_recv, x_send, x_recv):
    chan, tm = lax.axis_index("chan"), lax.axis_index("tm")
    half, member = tm // GROUP, tm % GROUP
    place = chan % ROW
    n_chan, n_tm = lax.axis_size("chan"), lax.axis_size("tm")

    def peer(o):
        return (chan, half * GROUP + lax.rem(member + o, GROUP))

    def beside(o):
        return (chan - place + lax.rem(place + o, ROW), tm)

    opposite = (chan, lax.rem(tm + GROUP, n_tm))
    above = (lax.rem(chan + ROW, n_chan), tm)
    below = (lax.rem(chan + n_chan - ROW, n_chan), tm)

    barrier = pltpu.get_barrier_semaphore()
    greeted = [peer(o) for o in range(1, GROUP)] + [beside(o) for o in range(1, ROW)]
    greeted += [opposite, above, below]
    for device in greeted:
        pl.semaphore_signal(barrier, inc=1, device_id=device, device_id_type=MESH)
    pl.semaphore_wait(barrier, len(greeted))

    def remote(src, dst, send, recv, device):
        return pltpu.make_async_remote_copy(
            src_ref=src, dst_ref=dst, send_sem=send, recv_sem=recv,
            device_id=device, device_id_type=MESH)

    def y_copy(j, o):
        to = lax.rem(member + o, GROUP)
        return remote(outgoing.at[j, to], incoming.at[j, member], y_send.at[j, o - 1],
                      y_recv.at[j, o - 1], peer(o))

    def self_copy(j):
        return pltpu.make_async_copy(outgoing.at[j, member], incoming.at[j, member], self_sem.at[j])

    def z_copy(j):
        return remote(crossing.at[j], both.at[0, j, pl.ds(GROUP, GROUP)], z_send.at[j], z_recv.at[j],
                      opposite)

    def spill_copy(j):
        return remote(incoming.at[j, GROUP - 1, 1, 1], spill.at[j], spill_send.at[j],
                      spill_recv.at[j], opposite)

    spans = (pl.ds(0, EARLY), pl.ds(EARLY, SLOTS - EARLY))

    def up_copy(j, part):
        return remote(both.at[0, j, spans[part]], both.at[1, j, spans[part]], up_send.at[j, part],
                      up_recv.at[j, part], above)

    def x_copy(j, part, o, item):
        return remote(both.at[item, j, spans[part]], others.at[o - 1, j, spans[part]],
                      x_send.at[j, part, o - 1], x_recv.at[j, part, o - 1], beside(o))

    def send_own(j, part):
        up_copy(j, part).start()
        for o in range(1, ROW):
            @pl.when(place + o < ROW)
            def _():
                x_copy(j, part, o, 0).start()

    def send_below(j, part):
        up_copy(j, part).wait_recv()
        for o in range(1, ROW):
            @pl.when(place + o >= ROW)
            def _():
                x_copy(j, part, o, 1).start()

    per_group = 4
    for group in range(LOCAL // per_group):
        first = group * per_group

        @pl.loop(0, CHANNELS // 16)
        def _(tile):
            rows = pl.ds(pl.multiple_of(tile * 16, 16), 16)
            for side in range(2):
                lanes = pl.ds(side * 128, 128)
                blocks = [
                    samples[rows, pl.ds(m * NFFT + side * 128, 128)].astype(jnp.float32)
                    for m in range(LOCAL)
                ]
                taps = [proto[k, :, lanes] for k in range(TAPS)]
                for i in range(per_group):
                    s = first + i
                    for part, members in ((0, range(s + 1)), (1, range(s + 1, LOCAL))):
                        pieces = []
                        for h in range(2):
                            total = None
                            for m in members:
                                k = TAPS - 1 - s + m if part == 0 else m - s - 1
                                term = taps[k] * blocks[m][h * 8:(h + 1) * 8]
                                total = term if total is None else total + term
                            if total is None:
                                total = jnp.zeros((8, 128), jnp.float32)
                            pieces.append(total)
                        frames[i, part, rows, lanes] = jnp.concatenate(pieces, 0).astype(jnp.bfloat16)

        @pl.loop(0, per_group)
        def _(i):
            for part in range(2):
                result = lax.dot_general(
                    fourier[...], frames[i, part], (((1,), (1,)), ((), ())),
                    preferred_element_type=jnp.float32)
                result = result.astype(jnp.bfloat16).reshape(2, GROUP, 16, CHANNELS)
                j = (first + i) // PER
                for h in range(2):
                    outgoing[j, :, h, part, i % PER] = result[h]

        for j in range(first // PER, (first + per_group) // PER):
            self_copy(j).start()
            for o in range(1, GROUP):
                y_copy(j, o).start()

    def gather(j):
        self_copy(j).wait()
        for o in range(1, GROUP):
            y_copy(j, o).wait_recv()

        def total(k, which):
            value = incoming[j, k, which, 0].astype(jnp.float32)
            if k > 0:
                value = value + incoming[j, k - 1, which, 1].astype(jnp.float32)
            return value.astype(jnp.bfloat16)

        for k in range(GROUP):
            crossing[j, k] = total(k, 1 - half)
        z_copy(j).start()

        @pl.when(half == 0)
        def _():
            spill_copy(j).start()

        for k in range(GROUP):
            both[0, j, k - 1 if k > 0 else EARLY] = total(k, half)
        send_own(j, 0)

    def join(j):
        z_copy(j).wait_recv()

        @pl.when(half == 0)
        def _():
            both[0, j, GROUP] = (both[0, j, GROUP].astype(jnp.float32)
                                 + incoming[j, GROUP - 1, 0, 1].astype(jnp.float32)
                                 ).astype(jnp.bfloat16)

        @pl.when(half == 1)
        def _():
            spill_copy(j).wait_recv()
            both[0, j, EARLY] = (both[0, j, EARLY].astype(jnp.float32)
                                 + spill[j].astype(jnp.float32)).astype(jnp.bfloat16)

        send_own(j, 1)

    def add_power(which, read):
        total = power[which]
        for k in range(SLOTS):
            for i in range(PER):
                value = read(k, i).astype(jnp.float32)
                total = total + value * value
        power[which] = total

    power[...] = jnp.zeros_like(power)

    @pl.loop(0, CHUNKS)
    def _(j):
        gather(j)

    @pl.loop(0, CHUNKS)
    def _(j):
        join(j)
        send_below(j, 0)
        send_below(j, 1)
        add_power(0, lambda k, i: both[0, j, k, i])
        for o in range(1, ROW):
            for part in range(2):
                x_copy(j, part, o, 0).wait_recv()
            add_power(o, lambda k, i: others[o - 1, j, k, i])

    def scale(which):
        total = power[which]
        mean = (total[:8] + total[8:]) * (1.0 / (2 * GROUP * LOCAL))
        factor = lax.rsqrt(mean + epsilon)
        return jnp.concatenate([factor, factor], 0)

    span = SLOTS * PER * 16

    own = scale(0)

    @pl.loop(0, CHUNKS)
    def _(j):
        value = both[0, j].astype(jnp.float32).reshape(SLOTS * PER, 16, CHANNELS) * own[None]
        flipped = jnp.concatenate([value[:, 8:], -value[:, :8]], 1)
        value = value.reshape(span, CHANNELS).astype(jnp.bfloat16)
        white[j] = value
        columns = pl.ds(pl.multiple_of(j * span, span), span)
        turned[0, :, columns] = value.T
        turned[1, :, columns] = flipped.reshape(span, CHANNELS).astype(jnp.bfloat16).T

    def correlate(distance):
        partner = white[...].reshape(CHUNKS * span, CHANNELS)
        for i in range(2):
            out[distance, i] = jnp.dot(
                turned[i], partner, preferred_element_type=jnp.float32) * (1.0 / (2 * GROUP * LOCAL))

    correlate(0)
    for o in range(1, ROW):
        factor = scale(o)

        @pl.loop(0, CHUNKS)
        def _(j):
            value = others[o - 1, j].astype(jnp.float32).reshape(SLOTS * PER, 16, CHANNELS)
            white[j] = (value * factor[None]).reshape(span, CHANNELS).astype(jnp.bfloat16)

        correlate(o)

    @pl.loop(0, CHUNKS)
    def _(j):
        for o in range(1, GROUP):
            y_copy(j, o).wait_send()
        z_copy(j).wait_send()

        @pl.when(half == 0)
        def _():
            spill_copy(j).wait_send()

        for part in range(2):
            up_copy(j, part).wait_send()
            for o in range(1, ROW):
                x_copy(j, part, o, 0).wait_send()


def on_device(samples):
    chunk = (SLOTS, PER, 16, CHANNELS)
    rows = CHUNKS * SLOTS * PER * 16
    dma = pltpu.SemaphoreType.DMA
    vmem = pl.BlockSpec(memory_space=pltpu.VMEM)
    bf16 = jnp.bfloat16
    result = pl.pallas_call(
        kernel,
        out_shape=jax.ShapeDtypeStruct((ROW, 2, CHANNELS, CHANNELS), jnp.float32),
        in_specs=[vmem] * 3,
        out_specs=vmem,
        scratch_shapes=[
            pltpu.VMEM((4, 2, CHANNELS, NFFT), bf16),
            pltpu.VMEM((CHUNKS, GROUP, 2, 2, PER, 16, CHANNELS), bf16),
            pltpu.VMEM((CHUNKS, GROUP, 2, 2, PER, 16, CHANNELS), bf16),
            pltpu.VMEM((2, CHUNKS) + chunk, bf16),
            pltpu.VMEM((CHUNKS, GROUP, PER, 16, CHANNELS), bf16),
            pltpu.VMEM((CHUNKS, PER, 16, CHANNELS), bf16),
            pltpu.VMEM((ROW - 1, CHUNKS) + chunk, bf16),
            pltpu.VMEM((ROW, 16, CHANNELS), jnp.float32),
            pltpu.VMEM((CHUNKS, rows // CHUNKS, CHANNELS), bf16),
            pltpu.VMEM((2, CHANNELS, rows), bf16),
            dma((CHUNKS, GROUP - 1)), dma((CHUNKS, GROUP - 1)), dma((CHUNKS,)),
            dma((CHUNKS,)), dma((CHUNKS,)), dma((CHUNKS,)), dma((CHUNKS,)),
            dma((CHUNKS, 2)), dma((CHUNKS, 2)),
            dma((CHUNKS, 2, ROW - 1)), dma((CHUNKS, 2, ROW - 1)),
        ],
        compiler_params=pltpu.CompilerParams(
            collective_id=0, has_side_effects=True, vmem_limit_bytes=50 * 2**20),
        cost_estimate=pl.CostEstimate(flops=5 * 10**9, bytes_accessed=4 * 2**20, transcendentals=0),
    )(samples, prototype(), transform_table())
    return result[None]


def solution(mesh):
    return jax.shard_map(
        on_device,
        mesh=mesh,
        in_specs=(P("chan", "tm"),),
        out_specs=P("tm", None, None, "chan", None),
        check_vma=False,
    )
```

```python
import math

import jax
import jax.numpy as jnp
import numpy as np
from jax import lax
from jax.experimental import pallas as pl
from jax.experimental.pallas import tpu as pltpu
from jax.sharding import PartitionSpec as P

NFFT = 256
TAPS = 16
BINS = 128
CHANNELS = 256
GROUP = 8
LOCAL = 16
CHUNKS = 8
PER = LOCAL // CHUNKS
SLOTS = 16
SPANS = ((0, 7), (7, 5), (12, 4))
AHEAD_Y = 2
AHEAD_Z = 1
STEPS = (2, 2, 4, 4, 4)
ROW = 4

epsilon = 1e-06
MESH = pl.DeviceIdType.MESH


def prototype():
    centred = (np.arange(TAPS * NFFT, dtype=np.float64) + 0.5 - 0.5 * TAPS * NFFT) / NFFT
    window = np.sinc(centred) * (0.5 + 0.5 * np.cos(2.0 * math.pi * centred / TAPS))
    table = window.reshape(TAPS, 1, NFFT).astype(np.float32)
    return np.broadcast_to(table, (TAPS, 8, NFFT)).copy()


def transform_table():
    frequency = np.arange(BINS)[:, None]
    phases = (frequency * np.arange(NFFT)[None, :] % NFFT) * (2.0 * math.pi / NFFT)
    parts = np.stack([np.cos(phases), -np.sin(phases)]).reshape(2, 16, 8, NFFT)
    return jnp.asarray(parts.transpose(1, 0, 2, 3).reshape(2 * BINS, NFFT), jnp.bfloat16)


def kernel(samples_hbm, proto_hbm, fourier_hbm, out, samples, proto, fourier, frames, outgoing,
           incoming, both, crossing, passing, spill, others, power, white, turned, in_sem, y_send,
           y_recv, self_sem, z_send, z_recv, hop_send, hop_recv, spill_send, spill_recv, up_send,
           up_recv, x_send, x_recv):
    chan, tm = lax.axis_index("chan"), lax.axis_index("tm")
    half, member = tm // GROUP, tm % GROUP
    place = chan % ROW
    n_chan, n_tm = lax.axis_size("chan"), lax.axis_size("tm")

    def peer(o):
        return (chan, half * GROUP + lax.rem(member + o, GROUP))

    def beside(o):
        return (chan - place + lax.rem(place + o, ROW), tm)

    opposite = (chan, lax.rem(tm + GROUP, n_tm))
    above = (lax.rem(chan + ROW, n_chan), tm)
    below = (lax.rem(chan + n_chan - ROW, n_chan), tm)

    far_above = (above[0], opposite[1])
    far_below = (below[0], opposite[1])

    inputs = [
        pltpu.make_async_copy(src, dst, in_sem.at[i])
        for i, (src, dst) in enumerate(
            ((samples_hbm, samples), (proto_hbm, proto), (fourier_hbm, fourier)))
    ]
    for copy in inputs:
        copy.start()
    barrier = pltpu.get_barrier_semaphore()
    greeted = [peer(o) for o in range(1, GROUP)] + [beside(o) for o in range(1, ROW)]
    greeted += [opposite, above, below, far_above, far_below]
    for device in greeted:
        pl.semaphore_signal(barrier, inc=1, device_id=device, device_id_type=MESH)
    pl.semaphore_wait(barrier, len(greeted))
    for copy in inputs:
        copy.wait()

    def remote(src, dst, send, recv, device):
        return pltpu.make_async_remote_copy(
            src_ref=src, dst_ref=dst, send_sem=send, recv_sem=recv,
            device_id=device, device_id_type=MESH)

    def y_copy(j, o):
        to = lax.rem(member + o, GROUP)
        return remote(outgoing.at[j, to], incoming.at[j, member], y_send.at[j, o - 1],
                      y_recv.at[j, o - 1], peer(o))

    def self_copy(j):
        return pltpu.make_async_copy(outgoing.at[j, member], incoming.at[j, member], self_sem.at[j])

    upper, lower = pl.ds(GROUP + 4, 4), pl.ds(GROUP, 4)

    def z_copy(j, way):
        if way == 0:
            return remote(crossing.at[j, pl.ds(4, 4)], both.at[1, j, upper], z_send.at[j, 0],
                          z_recv.at[j, 0], far_above)
        return remote(crossing.at[j, pl.ds(0, 4)], passing.at[j], z_send.at[j, 1], z_recv.at[j, 1],
                      far_below)

    def hop_copy(j, way):
        if way == 0:
            return remote(both.at[1, j, upper], both.at[0, j, upper], hop_send.at[j, 0],
                          hop_recv.at[j, 0], below)
        return remote(passing.at[j], both.at[0, j, lower], hop_send.at[j, 1], hop_recv.at[j, 1], above)

    def spill_copy(j):
        return remote(incoming.at[j, GROUP - 1, 1, 1], spill.at[j], spill_send.at[j],
                      spill_recv.at[j], opposite)

    spans = tuple(pl.ds(*span) for span in SPANS)

    def up_copy(j, part):
        return remote(both.at[0, j, spans[part]], both.at[1, j, spans[part]], up_send.at[j, part],
                      up_recv.at[j, part], above)

    def x_copy(j, part, o, item):
        return remote(both.at[item, j, spans[part]], others.at[o - 1, j, spans[part]],
                      x_send.at[j, part, o - 1], x_recv.at[j, part, o - 1], beside(o))

    def send_own(j, part):
        if part < 2:
            up_copy(j, part).start()
        for o in range(1, ROW):
            @pl.when(place + o < ROW)
            def _():
                x_copy(j, part, o, 0).start()

    def send_below(j, part):
        if part < 2:
            up_copy(j, part).wait_recv()
        for o in range(1, ROW):
            @pl.when(place + o >= ROW)
            def _():
                x_copy(j, part, o, 1).start()

    def relay(j, way):
        z_copy(j, way).wait_recv()
        hop_copy(j, way).start()
        if way == 0:
            send_below(j, 2)

    def transform(first, per_group):

        @pl.loop(0, CHANNELS // 16)
        def _(tile):
            rows = pl.ds(pl.multiple_of(tile * 16, 16), 16)
            for side in range(2):
                lanes = pl.ds(side * 128, 128)
                blocks = [
                    samples[rows, pl.ds(m * NFFT + side * 128, 128)].astype(jnp.float32)
                    for m in range(LOCAL)
                ]
                taps = [proto[k, :, lanes] for k in range(TAPS)]
                for i in range(per_group):
                    s = first + i
                    for part, members in ((0, range(s + 1)), (1, range(s + 1, LOCAL))):
                        pieces = []
                        for h in range(2):
                            total = None
                            for m in members:
                                k = TAPS - 1 - s + m if part == 0 else m - s - 1
                                term = taps[k] * blocks[m][h * 8:(h + 1) * 8]
                                total = term if total is None else total + term
                            if total is None:
                                total = jnp.zeros((8, 128), jnp.float32)
                            pieces.append(total)
                        frames[i, part, rows, lanes] = jnp.concatenate(pieces, 0).astype(jnp.bfloat16)

        @pl.loop(0, per_group)
        def _(i):
            for part in range(2):
                result = lax.dot_general(
                    fourier[...], frames[i, part], (((1,), (1,)), ((), ())),
                    preferred_element_type=jnp.float32)
                result = result.astype(jnp.bfloat16).reshape(2, GROUP, 16, CHANNELS)
                j = (first + i) // PER
                for h in range(2):
                    outgoing[j, :, h, part, i % PER] = result[h]

    def spread(j):
        self_copy(j).start()
        for o in range(1, GROUP):
            y_copy(j, o).start()

    def gather(j):
        self_copy(j).wait()
        for o in range(1, GROUP):
            y_copy(j, o).wait_recv()

        def total(k, which):
            value = incoming[j, k, which, 0].astype(jnp.float32)
            if k > 0:
                value = value + incoming[j, k - 1, which, 1].astype(jnp.float32)
            return value.astype(jnp.bfloat16)

        for k in range(GROUP):
            crossing[j, k] = total(k, 1 - half)
        for way in range(2):
            z_copy(j, way).start()

        @pl.when(half == 0)
        def _():
            spill_copy(j).start()

        for k in range(GROUP):
            both[0, j, k - 1 if k > 0 else GROUP - 1] = total(k, half)
        send_own(j, 0)

    def join(j):
        hop_copy(j, 1).wait_recv()

        @pl.when(half == 0)
        def _():
            both[0, j, GROUP] = (both[0, j, GROUP].astype(jnp.float32)
                                 + incoming[j, GROUP - 1, 0, 1].astype(jnp.float32)
                                 ).astype(jnp.bfloat16)

        @pl.when(half == 1)
        def _():
            spill_copy(j).wait_recv()
            both[0, j, GROUP - 1] = (both[0, j, GROUP - 1].astype(jnp.float32)
                                 + spill[j].astype(jnp.float32)).astype(jnp.bfloat16)

        send_own(j, 1)
        hop_copy(j, 0).wait_recv()
        send_own(j, 2)
        add_power(0, lambda k, i: both[0, j, k, i])

    def add_power(which, read):
        total = power[which]
        for k in range(SLOTS):
            for i in range(PER):
                value = read(k, i).astype(jnp.float32)
                total = total + value * value
        power[which] = total

    power[...] = jnp.zeros_like(power)

    def collect(j):
        for o in range(1, ROW):
            for part in range(len(SPANS)):
                x_copy(j, part, o, 0).wait_recv()
            add_power(o, lambda k, i: others[o - 1, j, k, i])

    first = spread_up_to = 0
    for count, step in enumerate(STEPS):
        if count == 2:
            gather(0)
        transform(first, step)
        first += step
        while spread_up_to < AHEAD_Y and (spread_up_to + 1) * PER <= first:
            spread(spread_up_to)
            spread_up_to += 1
    for j in range(1, AHEAD_Z):
        gather(j)

    @pl.loop(0, CHUNKS + 2)
    def _(j):
        @pl.when(j + AHEAD_Y < CHUNKS)
        def _():
            spread(j + AHEAD_Y)

        @pl.when(j + AHEAD_Z < CHUNKS)
        def _():
            gather(j + AHEAD_Z)

        @pl.when((j >= 1) & (j <= CHUNKS))
        def _():
            join(j - 1)

        @pl.when(j >= 2)
        def _():
            send_below(j - 2, 1)

        @pl.when(j < CHUNKS)
        def _():
            send_below(j, 0)
            for way in range(2):
                relay(j, way)

        @pl.when(j >= 3)
        def _():
            collect(j - 3)

    def scale(which):
        total = power[which]
        mean = (total[:8] + total[8:]) * (1.0 / (2 * GROUP * LOCAL))
        factor = lax.rsqrt(mean + epsilon)
        return jnp.concatenate([factor, factor], 0)

    span = SLOTS * PER * 16

    own = scale(0)

    @pl.loop(0, CHUNKS)
    def _(j):
        value = both[0, j].astype(jnp.float32).reshape(SLOTS * PER, 16, CHANNELS) * own[None]
        flipped = jnp.concatenate([value[:, 8:], -value[:, :8]], 1)
        value = value.reshape(span, CHANNELS).astype(jnp.bfloat16)
        white[j] = value
        columns = pl.ds(pl.multiple_of(j * span, span), span)
        turned[0, :, columns] = value.T
        turned[1, :, columns] = flipped.reshape(span, CHANNELS).astype(jnp.bfloat16).T

    def correlate(distance):
        partner = white[...].reshape(CHUNKS * span, CHANNELS)
        for i in range(2):
            out[distance, i] = jnp.dot(
                turned[i], partner, preferred_element_type=jnp.float32) * (1.0 / (2 * GROUP * LOCAL))

    correlate(0)
    collect(CHUNKS - 1)
    for o in range(1, ROW):
        factor = scale(o)

        @pl.loop(0, CHUNKS)
        def _(j):
            value = others[o - 1, j].astype(jnp.float32).reshape(SLOTS * PER, 16, CHANNELS)
            white[j] = (value * factor[None]).reshape(span, CHANNELS).astype(jnp.bfloat16)

        correlate(o)

    @pl.loop(0, CHUNKS)
    def _(j):
        for o in range(1, GROUP):
            y_copy(j, o).wait_send()
        for way in range(2):
            z_copy(j, way).wait_send()
            hop_copy(j, way).wait_send()

        @pl.when(half == 0)
        def _():
            spill_copy(j).wait_send()

        for part in range(len(SPANS)):
            if part < 2:
                up_copy(j, part).wait_send()
            for o in range(1, ROW):
                x_copy(j, part, o, 0).wait_send()


def on_device(samples):
    chunk = (SLOTS, PER, 16, CHANNELS)
    rows = CHUNKS * SLOTS * PER * 16
    dma = pltpu.SemaphoreType.DMA
    vmem = pl.BlockSpec(memory_space=pltpu.VMEM)
    bf16 = jnp.bfloat16
    result = pl.pallas_call(
        kernel,
        out_shape=jax.ShapeDtypeStruct((ROW, 2, CHANNELS, CHANNELS), jnp.float32),
        in_specs=[pl.BlockSpec(memory_space=pl.ANY)] * 3,
        out_specs=vmem,
        scratch_shapes=[
            pltpu.VMEM(samples.shape, bf16),
            pltpu.VMEM((TAPS, 8, NFFT), jnp.float32),
            pltpu.VMEM((2 * BINS, NFFT), bf16),
            pltpu.VMEM((max(STEPS), 2, CHANNELS, NFFT), bf16),
            pltpu.VMEM((CHUNKS, GROUP, 2, 2, PER, 16, CHANNELS), bf16),
            pltpu.VMEM((CHUNKS, GROUP, 2, 2, PER, 16, CHANNELS), bf16),
            pltpu.VMEM((2, CHUNKS) + chunk, bf16),
            pltpu.VMEM((CHUNKS, GROUP, PER, 16, CHANNELS), bf16),
            pltpu.VMEM((CHUNKS, GROUP // 2, PER, 16, CHANNELS), bf16),
            pltpu.VMEM((CHUNKS, PER, 16, CHANNELS), bf16),
            pltpu.VMEM((ROW - 1, CHUNKS) + chunk, bf16),
            pltpu.VMEM((ROW, 16, CHANNELS), jnp.float32),
            pltpu.VMEM((CHUNKS, rows // CHUNKS, CHANNELS), bf16),
            pltpu.VMEM((2, CHANNELS, rows), bf16),
            dma((3,)), dma((CHUNKS, GROUP - 1)), dma((CHUNKS, GROUP - 1)), dma((CHUNKS,)),
            dma((CHUNKS, 2)), dma((CHUNKS, 2)), dma((CHUNKS, 2)), dma((CHUNKS, 2)),
            dma((CHUNKS,)), dma((CHUNKS,)), dma((CHUNKS, 2)), dma((CHUNKS, 2)),
            dma((CHUNKS, len(SPANS), ROW - 1)), dma((CHUNKS, len(SPANS), ROW - 1)),
        ],
        compiler_params=pltpu.CompilerParams(
            collective_id=0, has_side_effects=True, vmem_limit_bytes=50 * 2**20),
        cost_estimate=pl.CostEstimate(flops=5 * 10**9, bytes_accessed=4 * 2**20, transcendentals=0),
    )(samples, prototype(), transform_table())
    return result[None]


def solution(mesh):
    return jax.shard_map(
        on_device,
        mesh=mesh,
        in_specs=(P("chan", "tm"),),
        out_specs=P("tm", None, None, "chan", None),
        check_vma=False,
    )
```

```python
import math

import jax
import jax.numpy as jnp
import numpy as np
from jax import lax
from jax.experimental import pallas as pl
from jax.experimental.pallas import tpu as pltpu
from jax.sharding import PartitionSpec as P

NFFT = 256
TAPS = 16
BINS = 128
CHANNELS = 256
GROUP = 8
LOCAL = 16
CHUNKS = 8
PER = LOCAL // CHUNKS
SLOTS = 16
SPANS = ((0, 7), (7, 5), (12, 4))
AHEAD_Y = 2
AHEAD_Z = 1
STEPS = (2, 2, 4, 4, 4)
ROW = 4

epsilon = 1e-06
MESH = pl.DeviceIdType.MESH


def prototype():
    centred = (np.arange(TAPS * NFFT, dtype=np.float64) + 0.5 - 0.5 * TAPS * NFFT) / NFFT
    window = np.sinc(centred) * (0.5 + 0.5 * np.cos(2.0 * math.pi * centred / TAPS))
    table = window.reshape(TAPS, 1, NFFT).astype(np.float32)
    return np.broadcast_to(table, (TAPS, 8, NFFT)).copy()


def transform_table():
    frequency = np.arange(BINS)[:, None]
    phases = (frequency * np.arange(NFFT)[None, :] % NFFT) * (2.0 * math.pi / NFFT)
    parts = np.stack([np.cos(phases), -np.sin(phases)]).reshape(2, 16, 8, NFFT)
    return jnp.asarray(parts.transpose(1, 0, 2, 3).reshape(2 * BINS, NFFT), jnp.bfloat16)


def kernel(samples_hbm, proto_hbm, fourier_hbm, out, samples, proto, fourier, frames, outgoing,
           incoming, both, crossing, passing, spill, others, power, white, turned, in_sem, y_send,
           y_recv, self_sem, z_send, z_recv, hop_send, hop_recv, spill_send, spill_recv, up_send,
           up_recv, x_send, x_recv):
    chan, tm = lax.axis_index("chan"), lax.axis_index("tm")
    half, member = tm // GROUP, tm % GROUP
    place = chan % ROW
    n_chan, n_tm = lax.axis_size("chan"), lax.axis_size("tm")

    def peer(o):
        return (chan, half * GROUP + lax.rem(member + o, GROUP))

    def beside(o):
        return (chan - place + lax.rem(place + o, ROW), tm)

    opposite = (chan, lax.rem(tm + GROUP, n_tm))
    above = (lax.rem(chan + ROW, n_chan), tm)
    below = (lax.rem(chan + n_chan - ROW, n_chan), tm)

    far_above = (above[0], opposite[1])
    far_below = (below[0], opposite[1])

    inputs = [
        pltpu.make_async_copy(src, dst, in_sem.at[i])
        for i, (src, dst) in enumerate(
            ((samples_hbm, samples), (proto_hbm, proto), (fourier_hbm, fourier)))
    ]
    for copy in inputs:
        copy.start()
    barrier = pltpu.get_barrier_semaphore()
    greeted = [peer(o) for o in range(1, GROUP)] + [beside(o) for o in range(1, ROW)]
    greeted += [opposite, above, below, far_above, far_below]
    for device in greeted:
        pl.semaphore_signal(barrier, inc=1, device_id=device, device_id_type=MESH)
    pl.semaphore_wait(barrier, len(greeted))
    for copy in inputs:
        copy.wait()

    def remote(src, dst, send, recv, device):
        return pltpu.make_async_remote_copy(
            src_ref=src, dst_ref=dst, send_sem=send, recv_sem=recv,
            device_id=device, device_id_type=MESH)

    def y_copy(j, o):
        to = lax.rem(member + o, GROUP)
        return remote(outgoing.at[j, to], incoming.at[j, member], y_send.at[j, o - 1],
                      y_recv.at[j, o - 1], peer(o))

    def self_copy(j):
        return pltpu.make_async_copy(outgoing.at[j, member], incoming.at[j, member], self_sem.at[j])

    upper, lower = pl.ds(GROUP + 4, 4), pl.ds(GROUP, 4)

    def z_copy(j, way):
        if way == 0:
            return remote(crossing.at[j, pl.ds(4, 4)], both.at[1, j, upper], z_send.at[j, 0],
                          z_recv.at[j, 0], far_above)
        return remote(crossing.at[j, pl.ds(0, 4)], passing.at[j], z_send.at[j, 1], z_recv.at[j, 1],
                      far_below)

    def hop_copy(j, way):
        if way == 0:
            return remote(both.at[1, j, upper], both.at[0, j, upper], hop_send.at[j, 0],
                          hop_recv.at[j, 0], below)
        return remote(passing.at[j], both.at[0, j, lower], hop_send.at[j, 1], hop_recv.at[j, 1], above)

    def spill_copy(j):
        return remote(incoming.at[j, GROUP - 1, 1, 1], spill.at[j], spill_send.at[j],
                      spill_recv.at[j], opposite)

    spans = tuple(pl.ds(*span) for span in SPANS)

    def up_copy(j, part):
        return remote(both.at[0, j, spans[part]], both.at[1, j, spans[part]], up_send.at[j, part],
                      up_recv.at[j, part], above)

    def x_copy(j, part, o, item):
        return remote(both.at[item, j, spans[part]], others.at[o - 1, j, spans[part]],
                      x_send.at[j, part, o - 1], x_recv.at[j, part, o - 1], beside(o))

    def send_own(j, part):
        if part < 2:
            up_copy(j, part).start()
        for o in range(1, ROW):
            @pl.when(place + o < ROW)
            def _():
                x_copy(j, part, o, 0).start()

    def send_below(j, part):
        if part < 2:
            up_copy(j, part).wait_recv()
        for o in range(1, ROW):
            @pl.when(place + o >= ROW)
            def _():
                x_copy(j, part, o, 1).start()

    def relay(j, way):
        z_copy(j, way).wait_recv()
        hop_copy(j, way).start()
        if way == 0:
            send_below(j, 2)

    def transform(first, per_group):

        @pl.loop(0, CHANNELS // 16)
        def _(tile):
            rows = pl.ds(pl.multiple_of(tile * 16, 16), 16)
            for side in range(2):
                lanes = pl.ds(side * 128, 128)
                blocks = [
                    samples[rows, pl.ds(m * NFFT + side * 128, 128)].astype(jnp.float32)
                    for m in range(LOCAL)
                ]
                taps = [proto[k, :, lanes] for k in range(TAPS)]
                for i in range(per_group):
                    s = first + i
                    for part, members in ((0, range(s + 1)), (1, range(s + 1, LOCAL))):
                        pieces = []
                        for h in range(2):
                            total = None
                            for m in members:
                                k = TAPS - 1 - s + m if part == 0 else m - s - 1
                                term = taps[k] * blocks[m][h * 8:(h + 1) * 8]
                                total = term if total is None else total + term
                            if total is None:
                                total = jnp.zeros((8, 128), jnp.float32)
                            pieces.append(total)
                        frames[i, part, rows, lanes] = jnp.concatenate(pieces, 0).astype(jnp.bfloat16)

        @pl.loop(0, per_group)
        def _(i):
            for part in range(2):
                result = lax.dot_general(
                    fourier[...], frames[i, part], (((1,), (1,)), ((), ())),
                    preferred_element_type=jnp.float32)
                result = result.astype(jnp.bfloat16).reshape(2, GROUP, 16, CHANNELS)
                j = (first + i) // PER
                for h in range(2):
                    outgoing[j, :, h, part, i % PER] = result[h]

    def spread(j):
        self_copy(j).start()
        for o in range(1, GROUP):
            y_copy(j, o).start()

    def gather(j):
        self_copy(j).wait()
        for o in range(1, GROUP):
            y_copy(j, o).wait_recv()

        def total(k, which):
            value = incoming[j, k, which, 0].astype(jnp.float32)
            if k > 0:
                value = value + incoming[j, k - 1, which, 1].astype(jnp.float32)
            return value.astype(jnp.bfloat16)

        for k in range(GROUP):
            crossing[j, k] = total(k, 1 - half)
        for way in range(2):
            z_copy(j, way).start()

        @pl.when(half == 0)
        def _():
            spill_copy(j).start()

        for k in range(GROUP):
            both[0, j, k - 1 if k > 0 else GROUP - 1] = total(k, half)
        send_own(j, 0)

    def join(j):
        hop_copy(j, 1).wait_recv()

        @pl.when(half == 0)
        def _():
            both[0, j, GROUP] = (both[0, j, GROUP].astype(jnp.float32)
                                 + incoming[j, GROUP - 1, 0, 1].astype(jnp.float32)
                                 ).astype(jnp.bfloat16)

        @pl.when(half == 1)
        def _():
            spill_copy(j).wait_recv()
            both[0, j, GROUP - 1] = (both[0, j, GROUP - 1].astype(jnp.float32)
                                 + spill[j].astype(jnp.float32)).astype(jnp.bfloat16)

        send_own(j, 1)
        hop_copy(j, 0).wait_recv()
        send_own(j, 2)
        add_power(0, lambda k, i: both[0, j, k, i])

    def add_power(which, read):
        total = power[which]
        for k in range(SLOTS):
            for i in range(PER):
                value = read(k, i).astype(jnp.float32)
                total = total + value * value
        power[which] = total

    power[...] = jnp.zeros_like(power)

    def collect(j):
        for o in range(1, ROW):
            for part in range(len(SPANS)):
                x_copy(j, part, o, 0).wait_recv()
            add_power(o, lambda k, i: others[o - 1, j, k, i])

    first = spread_up_to = 0
    for count, step in enumerate(STEPS):
        if count == 2:
            gather(0)
        transform(first, step)
        first += step
        while spread_up_to < AHEAD_Y and (spread_up_to + 1) * PER <= first:
            spread(spread_up_to)
            spread_up_to += 1
    for j in range(1, AHEAD_Z):
        gather(j)

    @pl.loop(0, CHUNKS + 2)
    def _(j):
        @pl.when(j + AHEAD_Y < CHUNKS)
        def _():
            spread(j + AHEAD_Y)

        @pl.when(j + AHEAD_Z < CHUNKS)
        def _():
            gather(j + AHEAD_Z)

        @pl.when(j < CHUNKS)
        def _():
            send_below(j, 0)
            for way in range(2):
                relay(j, way)

        @pl.when((j >= 1) & (j <= CHUNKS))
        def _():
            join(j - 1)

        @pl.when(j >= 2)
        def _():
            send_below(j - 2, 1)

        @pl.when(j >= 3)
        def _():
            collect(j - 3)

    def scale(which):
        total = power[which]
        mean = (total[:8] + total[8:]) * (1.0 / (2 * GROUP * LOCAL))
        factor = lax.rsqrt(mean + epsilon)
        return jnp.concatenate([factor, factor], 0)

    span = SLOTS * PER * 16

    own = scale(0)

    @pl.loop(0, CHUNKS)
    def _(j):
        value = both[0, j].astype(jnp.float32).reshape(SLOTS * PER, 16, CHANNELS) * own[None]
        flipped = jnp.concatenate([value[:, 8:], -value[:, :8]], 1)
        value = value.reshape(span, CHANNELS).astype(jnp.bfloat16)
        white[j] = value
        columns = pl.ds(pl.multiple_of(j * span, span), span)
        turned[0, :, columns] = value.T
        turned[1, :, columns] = flipped.reshape(span, CHANNELS).astype(jnp.bfloat16).T

    def correlate(distance):
        partner = white[...].reshape(CHUNKS * span, CHANNELS)
        for i in range(2):
            out[distance, i] = jnp.dot(
                turned[i], partner, preferred_element_type=jnp.float32) * (1.0 / (2 * GROUP * LOCAL))

    correlate(0)
    collect(CHUNKS - 1)
    for o in range(1, ROW):
        factor = scale(o)

        @pl.loop(0, CHUNKS)
        def _(j):
            value = others[o - 1, j].astype(jnp.float32).reshape(SLOTS * PER, 16, CHANNELS)
            white[j] = (value * factor[None]).reshape(span, CHANNELS).astype(jnp.bfloat16)

        correlate(o)

    @pl.loop(0, CHUNKS)
    def _(j):
        for o in range(1, GROUP):
            y_copy(j, o).wait_send()
        for way in range(2):
            z_copy(j, way).wait_send()
            hop_copy(j, way).wait_send()

        @pl.when(half == 0)
        def _():
            spill_copy(j).wait_send()

        for part in range(len(SPANS)):
            if part < 2:
                up_copy(j, part).wait_send()
            for o in range(1, ROW):
                x_copy(j, part, o, 0).wait_send()


def on_device(samples):
    chunk = (SLOTS, PER, 16, CHANNELS)
    rows = CHUNKS * SLOTS * PER * 16
    dma = pltpu.SemaphoreType.DMA
    vmem = pl.BlockSpec(memory_space=pltpu.VMEM)
    bf16 = jnp.bfloat16
    result = pl.pallas_call(
        kernel,
        out_shape=jax.ShapeDtypeStruct((ROW, 2, CHANNELS, CHANNELS), jnp.float32),
        in_specs=[pl.BlockSpec(memory_space=pl.ANY)] * 3,
        out_specs=vmem,
        scratch_shapes=[
            pltpu.VMEM(samples.shape, bf16),
            pltpu.VMEM((TAPS, 8, NFFT), jnp.float32),
            pltpu.VMEM((2 * BINS, NFFT), bf16),
            pltpu.VMEM((max(STEPS), 2, CHANNELS, NFFT), bf16),
            pltpu.VMEM((CHUNKS, GROUP, 2, 2, PER, 16, CHANNELS), bf16),
            pltpu.VMEM((CHUNKS, GROUP, 2, 2, PER, 16, CHANNELS), bf16),
            pltpu.VMEM((2, CHUNKS) + chunk, bf16),
            pltpu.VMEM((CHUNKS, GROUP, PER, 16, CHANNELS), bf16),
            pltpu.VMEM((CHUNKS, GROUP // 2, PER, 16, CHANNELS), bf16),
            pltpu.VMEM((CHUNKS, PER, 16, CHANNELS), bf16),
            pltpu.VMEM((ROW - 1, CHUNKS) + chunk, bf16),
            pltpu.VMEM((ROW, 16, CHANNELS), jnp.float32),
            pltpu.VMEM((CHUNKS, rows // CHUNKS, CHANNELS), bf16),
            pltpu.VMEM((2, CHANNELS, rows), bf16),
            dma((3,)), dma((CHUNKS, GROUP - 1)), dma((CHUNKS, GROUP - 1)), dma((CHUNKS,)),
            dma((CHUNKS, 2)), dma((CHUNKS, 2)), dma((CHUNKS, 2)), dma((CHUNKS, 2)),
            dma((CHUNKS,)), dma((CHUNKS,)), dma((CHUNKS, 2)), dma((CHUNKS, 2)),
            dma((CHUNKS, len(SPANS), ROW - 1)), dma((CHUNKS, len(SPANS), ROW - 1)),
        ],
        compiler_params=pltpu.CompilerParams(
            collective_id=0, has_side_effects=True, vmem_limit_bytes=50 * 2**20),
        cost_estimate=pl.CostEstimate(flops=5 * 10**9, bytes_accessed=4 * 2**20, transcendentals=0),
    )(samples, prototype(), transform_table())
    return result[None]


def solution(mesh):
    return jax.shard_map(
        on_device,
        mesh=mesh,
        in_specs=(P("chan", "tm"),),
        out_specs=P("tm", None, None, "chan", None),
        check_vma=False,
    )
```
